32 devices in a mesh: ctx: 8 (over y, x, core), ch: 4 (over z).
Axes of the slice: x: 2, y: 2, z: 4, core: 2. Of those that a mesh axis runs over, the one named last changes fastest.
Arguments:
- queries: bfloat16 [1024, 4096], P('ctx', 'ch'), may hold values from -6 to 6
- keys: bfloat16 [1024, 4096], P('ctx', 'ch'), may hold values from -6 to 6
- values: bfloat16 [1024, 4096], P('ctx', 'ch'), may hold values from -6 to 6
- grad_out: bfloat16 [1024, 4096], P('ctx', 'ch'), may hold values from -6 to 6
- residues: float32 [4096, 16], P('ch'), may hold values from -0.1875 to 0.1875
- decays: float32 [4096, 16], P('ch'), may hold values from 0.0009765625 to 0.03
- skip: float32 [4096], P('ch'), may hold values from -6 to 6
Outputs:
- query_grad: bfloat16 [1024, 4096], P('ctx', 'ch')
- key_grad: bfloat16 [1024, 4096], P('ctx', 'ch')
- value_grad: bfloat16 [1024, 4096], P('ctx', 'ch')
- residue_grad: float32 [4096, 16], P('ch')
- decay_grad: float32 [4096, 16], P('ch')
The draws below stay inside these ranges and needn't reach their ends.
All inputs are finite; a program needn't handle non-finite values.
Results may differ from the reference program's by a relative error of at most 0.001.
Values sent between devices are 32-bit elements; how exact they have to be, the bound alone decides.
A program may use at most 128 MiB of HBM per device.

```python
import math
import jax
import jax.numpy as jnp
from jax import lax

D = 4096
M = 16
SEQ = 1024


def levels(rng, extent, split, smallest, largest):
    def one(axis_at, shards_of):
        draws = jax.random.uniform(jax.random.fold_in(jax.random.fold_in(rng, 6), axis_at), (shards_of,), jnp.float32, smallest / len(split), largest / len(split))
        return jnp.repeat(jnp.exp(draws), extent[axis_at] // shards_of).reshape((-1,) + (1,) * (len(extent) - axis_at - 1))

    level = one(*split[0])
    for cut in split[1:]:
        level = level * one(*cut)
    return level


def noise(rng, shape, scale, reach, cuts=(), held_as=jnp.bfloat16):
    drawn = jax.random.normal(rng, shape, jnp.float32) * scale
    if len(cuts) > 0:
        drawn = levels(rng, shape, cuts, -0.22, 0.18) * drawn
    return jnp.clip(drawn, min=-reach, max=reach).astype(held_as)


def setup_inputs(seed: int = 0) -> dict:
    seeds = jax.random.split(jax.random.key(seed), 8)
    queries = noise(seeds[0], (SEQ, D), 1.0, 6.0, ((0, 8), (1, 4)))
    keys = noise(seeds[1], (SEQ, D), 1.0, 6.0, ((0, 8), (1, 4)))
    values = noise(seeds[2], (SEQ, D), 1.0, 6.0, ((0, 8), (1, 4)))
    grad_out = noise(seeds[3], (SEQ, D), 1.0, 6.0, ((0, 8), (1, 4)))
    residues = noise(seeds[4], (D, M), (M * SEQ // 16) ** -0.5, 0.1875, ((0, 4),), jnp.float32)
    decays = jnp.clip(jnp.exp(math.log(0.03) - 3.424914 * jax.random.uniform(seeds[5], (D, M), jnp.float32) ** levels(seeds[5], (D, M), ((0, 4),), -0.2, 0.2)), 0.0009765625, 0.03)
    skip = noise(seeds[6], (D,), 1.0, 6.0, ((0, 4),), jnp.float32)
    return {"queries": queries, "keys": keys, "values": values, "grad_out": grad_out, "residues": residues, "decays": decays, "skip": skip}


def reference(queries, keys, values, grad_out, residues, decays, skip):
    seq_len, width = queries.shape
    pole_count = residues.shape[1]
    group_width = math.gcd(width, 256)
    group_count = width // group_width
    length = 2 * seq_len
    positions = jnp.arange(seq_len).astype(jnp.float32)

    def by_group(array):
        return array.reshape(seq_len, group_count, group_width).transpose(1, 0, 2)

    def per_group(group):
        q_part, k_part, v_part, g_part, res_part, dec_part, skip_part = group
        signal = k_part.astype(jnp.float32) * v_part.astype(jnp.float32)
        outer = q_part.astype(jnp.float32) * g_part.astype(jnp.float32)
        decay_table = jnp.exp(-positions[:, None, None] * dec_part[None, :, :])
        kernel = jnp.einsum("tcm,cm->tc", decay_table, res_part, precision=lax.Precision.HIGHEST)
        signal_hat = jnp.fft.rfft(signal, n=length, axis=0)
        outer_hat = jnp.fft.rfft(outer, n=length, axis=0)
        kernel_hat = jnp.fft.rfft(kernel, n=length, axis=0)
        conv = jnp.fft.irfft(kernel_hat * signal_hat, n=length, axis=0)[:seq_len] + skip_part * signal
        adjoint = jnp.fft.irfft(jnp.conj(kernel_hat) * outer_hat, n=length, axis=0)[:seq_len] + skip_part * outer
        kernel_grad = jnp.fft.irfft(jnp.conj(signal_hat) * outer_hat, n=length, axis=0)[:seq_len]
        res_grad = jnp.einsum("tc,tcm->cm", kernel_grad, decay_table, precision=lax.Precision.HIGHEST) / seq_len
        dec_grad = jnp.einsum("tc,tcm->cm", kernel_grad * positions[:, None], decay_table, precision=lax.Precision.HIGHEST) * dec_part / seq_len
        query_grad = (g_part.astype(jnp.float32) * conv).astype(jnp.bfloat16)
        key_grad = (adjoint * v_part.astype(jnp.float32)).astype(jnp.bfloat16)
        value_grad = (adjoint * k_part.astype(jnp.float32)).astype(jnp.bfloat16)
        return query_grad, key_grad, value_grad, res_grad, dec_grad

    results = lax.map(per_group, (by_group(queries), by_group(keys), by_group(values), by_group(grad_out),
                                  residues.reshape(group_count, group_width, pole_count),
                                  decays.reshape(group_count, group_width, pole_count),
                                  skip.reshape(group_count, group_width)))

    def unite(array):
        return array.transpose(1, 0, 2).reshape(seq_len, width)

    return (unite(results[0]), unite(results[1]), unite(results[2]),
            results[3].reshape(width, pole_count), results[4].reshape(width, pole_count))
```

```python
import functools

import jax
import jax.numpy as jnp
from jax import lax
from jax.experimental import pallas as pl
from jax.experimental.pallas import tpu as pltpu
from jax.sharding import PartitionSpec as P

LANES = 128
SUB = 8
MESH = pl.DeviceIdType.MESH
f32 = jnp.float32


def kernel(
    n, own, q_ref, k_ref, v_ref, g_ref, res_ref, dec_ref, skip_ref,
    qg_ref, kg_ref, vg_ref, rg_ref, dg_ref,
    u_s, o_s, conv_s, adj_s, d_s, a_s, w_s, rt_s, dt_s, send1, got1, send2, got2,
    ss1, rs1, ss2, rs2,
):
    rows, cols = q_ref.shape
    modes = res_ref.shape[1]
    groups = cols // LANES
    seq = rows * n
    slab = modes * groups // own
    per = slab // SUB
    me = lax.axis_index("ctx")

    barrier = pltpu.get_barrier_semaphore()

    @pl.loop(0, n)
    def _(peer):
        @pl.when(peer != me)
        def _():
            pl.semaphore_signal(barrier, inc=1, device_id={"ctx": peer}, device_id_type=MESH)

    for g in range(groups):
        lanes = slice(g * LANES, (g + 1) * LANES)
        block = slice(g * rows, (g + 1) * rows)
        u = k_ref[:, lanes].astype(f32) * v_ref[:, lanes].astype(f32)
        o = q_ref[:, lanes].astype(f32) * g_ref[:, lanes].astype(f32)
        skip = skip_ref[:, lanes]
        u_s[block, :] = u
        o_s[block, :] = o
        conv_s[block, :] = skip * u
        adj_s[block, :] = skip * o
        d = dec_ref[lanes, :].T
        d_s[pl.ds(g, modes, stride=groups), :] = d
        a_s[pl.ds(g, modes, stride=groups), :] = jnp.exp(-d)
        w_s[pl.ds(g, modes, stride=groups), :] = res_ref[lanes, :].T

    def at(ref, t):
        return ref.at[pl.ds(t, SUB, stride=rows), :]

    def mode_rows(m):
        return pl.ds(pl.multiple_of(m * SUB, SUB), SUB)

    pl.semaphore_wait(barrier, n - 1)

    zero = jnp.zeros((SUB, LANES), f32)
    batch = 4
    turns = modes // batch
    owners_per = batch // per
    unroll = 8

    def to_owner(q):
        return pltpu.make_async_remote_copy(
            src_ref=send1.at[q], dst_ref=got1.at[me], send_sem=ss1.at[q], recv_sem=rs1.at[me],
            device_id={"ctx": q}, device_id_type=MESH)

    @pl.loop(0, turns)
    def _(turn):
        c = lax.rem(turn + me // owners_per, turns)
        a = [a_s[mode_rows(c * batch + j), :] for j in range(batch)]

        def step(i, carry):
            x, y, r, e, z, v = [list(s) for s in carry]
            for k in range(unroll):
                t = i * unroll + k
                ut = at(u_s, t)[...]
                ot = at(o_s, t)[...]
                ob = at(o_s, rows - 1 - t)[...]
                for j in range(batch):
                    y[j] = a[j] * (y[j] + x[j])
                    x[j] = a[j] * x[j] + ut
                    r[j] = r[j] + ot * x[j]
                    e[j] = e[j] + ot * y[j]
                    z[j] = a[j] * z[j] + ob
                    v[j] = a[j] * v[j] + z[j]
            return tuple(tuple(s) for s in (x, y, r, e, z, v))

        done = lax.fori_loop(0, rows // unroll, step, tuple((zero,) * batch for _ in range(6)))
        for j in range(batch):
            for f in range(6):
                send1[c * owners_per + j // per, f, (j % per) * SUB:(j % per + 1) * SUB, :] = done[f][j]
        for b in range(owners_per):
            q = c * owners_per + b

            @pl.when(q != me)
            def _():
                to_owner(q).start()

    batch2 = 8

    @pl.loop(0, modes // batch2)
    def _(c):
        a = [a_s[mode_rows(c * batch2 + j), :] for j in range(batch2)]
        w = [w_s[mode_rows(c * batch2 + j), :] for j in range(batch2)]

        def step(i, carry):
            x, z = [list(s) for s in carry]
            for k in range(unroll):
                t = i * unroll + k
                b = rows - 1 - t
                ut = at(u_s, t)[...]
                ob = at(o_s, b)[...]
                cs = []
                zs = []
                for j in range(batch2):
                    x[j] = a[j] * x[j] + ut
                    z[j] = a[j] * z[j] + ob
                    cs.append(w[j] * x[j])
                    zs.append(w[j] * z[j])
                while len(cs) > 1:
                    cs = [p + q for p, q in zip(cs[::2], cs[1::2])]
                    zs = [p + q for p, q in zip(zs[::2], zs[1::2])]
                at(conv_s, t)[...] = at(conv_s, t)[...] + cs[0]
                at(adj_s, b)[...] = at(adj_s, b)[...] + zs[0]
            return tuple(x), tuple(z)

        lax.fori_loop(0, rows // unroll, step, ((zero,) * batch2, (zero,) * batch2))

    def from_peer(r):
        return pltpu.make_async_remote_copy(
            src_ref=send1.at[0], dst_ref=got1.at[r], send_sem=ss1.at[0], recv_sem=rs1.at[r],
            device_id={"ctx": r}, device_id_type=MESH)

    def back(r):
        return pltpu.make_async_remote_copy(
            src_ref=send2.at[r], dst_ref=got2.at[me], send_sem=ss2.at[r], recv_sem=rs2.at[me],
            device_id={"ctx": r}, device_id_type=MESH)

    def from_owner(q):
        return pltpu.make_async_remote_copy(
            src_ref=send2.at[0], dst_ref=got2.at[q], send_sem=ss2.at[0], recv_sem=rs2.at[q],
            device_id={"ctx": q}, device_id_type=MESH)

    @pl.when(me < own)
    def _():
        got1[me] = send1[me]

        @pl.loop(0, n)
        def _(r):
            @pl.when(r != me)
            def _():
                from_peer(r).wait_recv()

        mine = pl.ds(pl.multiple_of(me * slab, slab), slab)
        d = d_s[mine, :]
        a = a_s[mine, :]
        at_end = jnp.exp(-float(rows) * d)
        none = jnp.zeros((slab, LANES), f32)

        def ahead(r, carry):
            x, y, rt, dt = carry
            send2[r, 0] = x
            z, v = got1[r, 4], got1[r, 5]
            rt = rt + got1[r, 2] + a * (x * z)
            dt = dt + got1[r, 3] + a * (v * x + z * y)
            y = at_end * (y + float(rows) * x) + got1[r, 1]
            x = at_end * x + got1[r, 0]
            return x, y, rt, dt

        few = n <= 16
        _, _, rt, dt = lax.fori_loop(0, n, ahead, (none,) * 4, unroll=few)
        rt = rt / seq
        dt = dt * d / seq

        def behind(i, z):
            r = n - 1 - i
            send2[r, 1] = z
            send2[r, 2] = rt
            send2[r, 3] = dt
            z = at_end * z + got1[r, 4]
            return z

        lax.fori_loop(0, n, behind, none, unroll=few)

        @pl.loop(0, n)
        def _(r):
            @pl.when(r != me)
            def _():
                back(r).start()

        got2[me] = send2[me]

    @pl.loop(0, own)
    def _(q):
        @pl.when(q != me)
        def _():
            from_owner(q).wait_recv()

    @pl.loop(0, modes // batch2)
    def _(c):
        a, p, s = [], [], []
        for j in range(batch2):
            m = c * batch2 + j
            aj = a_s[mode_rows(m), :]
            wa = w_s[mode_rows(m), :] * aj
            q = m // per
            sub = pl.ds(pl.multiple_of((m % per) * SUB, SUB), SUB)
            a.append(aj)
            p.append(wa * got2[q, 0, sub, :])
            s.append(wa * got2[q, 1, sub, :])
            rt_s[mode_rows(m), :] = got2[q, 2, sub, :]
            dt_s[mode_rows(m), :] = got2[q, 3, sub, :]

        def step(i, carry):
            p, s = [list(x) for x in carry]
            for k in range(unroll):
                t = i * unroll + k
                b = rows - 1 - t
                cs, zs = list(p), list(s)
                while len(cs) > 1:
                    cs = [x + y for x, y in zip(cs[::2], cs[1::2])]
                    zs = [x + y for x, y in zip(zs[::2], zs[1::2])]
                at(conv_s, t)[...] = at(conv_s, t)[...] + cs[0]
                at(adj_s, b)[...] = at(adj_s, b)[...] + zs[0]
                p = [x * y for x, y in zip(a, p)]
                s = [x * y for x, y in zip(a, s)]
            return tuple(p), tuple(s)

        lax.fori_loop(0, rows // unroll, step, (tuple(p), tuple(s)))

    for g in range(groups):
        lanes = slice(g * LANES, (g + 1) * LANES)
        block = slice(g * rows, (g + 1) * rows)
        adj = adj_s[block, :]
        qg_ref[:, lanes] = (g_ref[:, lanes].astype(f32) * conv_s[block, :]).astype(qg_ref.dtype)
        kg_ref[:, lanes] = (adj * v_ref[:, lanes].astype(f32)).astype(kg_ref.dtype)
        vg_ref[:, lanes] = (adj * k_ref[:, lanes].astype(f32)).astype(vg_ref.dtype)
        rg_ref[lanes, :] = rt_s[pl.ds(g, modes, stride=groups), :].T
        dg_ref[lanes, :] = dt_s[pl.ds(g, modes, stride=groups), :].T

    @pl.loop(0, own)
    def _(q):
        @pl.when(q != me)
        def _():
            to_owner(q).wait_send()

    @pl.when(me < own)
    def _():
        @pl.loop(0, n)
        def _(r):
            @pl.when(r != me)
            def _():
                back(r).wait_send()


def body(n, queries, keys, values, grad_out, residues, decays, skip):
    rows, cols = queries.shape
    modes = residues.shape[1]
    own = min(n, modes)
    slab = modes * cols // LANES // own
    vmem = pl.BlockSpec(memory_space=pltpu.VMEM)
    field = pltpu.VMEM((rows * cols // LANES, LANES), f32)
    table = pltpu.VMEM((modes * cols // LANES, LANES), f32)
    grads = jax.ShapeDtypeStruct((rows, cols), jnp.bfloat16)
    sums = jax.ShapeDtypeStruct((cols, modes), f32)
    return pl.pallas_call(
        functools.partial(kernel, n, own),
        out_shape=(grads, grads, grads, sums, sums),
        in_specs=[vmem] * 7,
        out_specs=(vmem,) * 5,
        scratch_shapes=[
            field, field, field, field,
            table, table, table, table, table,
            pltpu.VMEM((own, 6, slab, LANES), f32),
            pltpu.VMEM((n, 6, slab, LANES), f32),
            pltpu.VMEM((n, 4, slab, LANES), f32),
            pltpu.VMEM((own, 4, slab, LANES), f32),
            pltpu.SemaphoreType.DMA((own,)),
            pltpu.SemaphoreType.DMA((n,)),
            pltpu.SemaphoreType.DMA((n,)),
            pltpu.SemaphoreType.DMA((own,)),
        ],
        compiler_params=pltpu.CompilerParams(
            collective_id=0, has_side_effects=True, vmem_limit_bytes=40 * 1024 * 1024
        ),
    )(queries, keys, values, grad_out, residues, decays, skip.reshape(1, cols))


def solution(mesh):
    return jax.shard_map(
        functools.partial(body, mesh.shape["ctx"]),
        mesh=mesh,
        in_specs=(
            P("ctx", "ch"), P("ctx", "ch"), P("ctx", "ch"), P("ctx", "ch"),
            P("ch", None), P("ch", None), P("ch"),
        ),
        out_specs=(P("ctx", "ch"), P("ctx", "ch"), P("ctx", "ch"), P("ch", None), P("ch", None)),
        check_vma=False,
    )
```

```python
import functools

import jax
import jax.numpy as jnp
from jax import lax
from jax.experimental import pallas as pl
from jax.experimental.pallas import tpu as pltpu
from jax.sharding import PartitionSpec as P

LANES = 128
SUB = 8
MESH = pl.DeviceIdType.MESH
f32 = jnp.float32


def kernel(
    n, own, q_hbm, k_hbm, v_hbm, g_hbm, res_hbm, dec_hbm, skip_hbm,
    conv_out, adj_out, rt_s, dt_s,
    q_ref, k_ref, v_ref, g_ref, res_ref, dec_ref, skip_ref, ins,
    u_s, o_s, conv_s, adj_s, d_s, a_s, w_s,
    ends, got_ends, sums, got_sums, starts, got_starts, totals, got_totals,
    ends_out, ends_in, sums_out, sums_in, starts_out, starts_in, totals_out, totals_in,
):
    rows, cols = q_ref.shape
    modes = res_ref.shape[0]
    groups = cols // LANES
    seq = rows * n
    slab = modes * groups // own
    per = slab // SUB
    me = lax.axis_index("ctx")

    barrier = pltpu.get_barrier_semaphore()
    fetches = [
        pltpu.make_async_copy(src, dst, ins.at[i])
        for i, (src, dst) in enumerate((
            (dec_hbm, dec_ref), (k_hbm, k_ref), (v_hbm, v_ref), (q_hbm, q_ref),
            (g_hbm, g_ref), (res_hbm, res_ref), (skip_hbm, skip_ref)))
    ]
    for fetch in fetches:
        fetch.start()

    @pl.loop(0, n)
    def _(peer):
        @pl.when(peer != me)
        def _():
            pl.semaphore_signal(barrier, inc=1, device_id={"ctx": peer}, device_id_type=MESH)

    for fetch in fetches:
        fetch.wait()
    for g in range(groups):
        lanes = slice(g * LANES, (g + 1) * LANES)
        block = slice(g * rows, (g + 1) * rows)
        u_s[block, :] = k_ref[:, lanes].astype(f32) * v_ref[:, lanes].astype(f32)
        o_s[block, :] = q_ref[:, lanes].astype(f32) * g_ref[:, lanes].astype(f32)
        d = dec_ref[:, lanes]
        d_s[pl.ds(g, modes, stride=groups), :] = d
        a_s[pl.ds(g, modes, stride=groups), :] = jnp.exp(-d)
        w_s[pl.ds(g, modes, stride=groups), :] = res_ref[:, lanes]

    def at(ref, t):
        return ref.at[pl.ds(t, SUB, stride=rows), :]

    def mode_rows(m):
        return pl.ds(pl.multiple_of(m * SUB, SUB), SUB)

    def link(src, dst, sent, landed, peer):
        return pltpu.make_async_remote_copy(
            src_ref=src, dst_ref=dst, send_sem=sent, recv_sem=landed,
            device_id={"ctx": peer}, device_id_type=MESH)

    def each_other(count, act):
        @pl.loop(0, count)
        def _(i):
            @pl.when(i != me)
            def _():
                act(i)

    def ends_to(q):
        return link(ends.at[q], got_ends.at[me], ends_out.at[q], ends_in.at[me], q)

    def ends_from(r):
        return link(ends.at[0], got_ends.at[r], ends_out.at[0], ends_in.at[r], r)

    def sums_to(q):
        return link(sums.at[q], got_sums.at[me], sums_out.at[q], sums_in.at[me], q)

    def sums_from(r):
        return link(sums.at[0], got_sums.at[r], sums_out.at[0], sums_in.at[r], r)

    def starts_to(r):
        return link(starts.at[r], got_starts.at[me], starts_out.at[r], starts_in.at[me], r)

    def starts_from(q):
        return link(starts.at[0], got_starts.at[q], starts_out.at[0], starts_in.at[q], q)

    def totals_to(r):
        return link(totals, got_totals.at[me], totals_out.at[r], totals_in.at[me], r)

    def totals_from(q):
        return link(totals, got_totals.at[q], totals_out.at[0], totals_in.at[q], q)

    zero = jnp.zeros((SUB, LANES), f32)
    batch = 4
    turns = modes // batch
    owners_per = batch // per
    unroll = 8

    def chunk_of(turn):
        return lax.rem(turn + me // owners_per, turns)

    wide = 16

    def edges(c):
        a = [a_s[mode_rows(c * wide + j), :] for j in range(wide)]

        def step(i, carry):
            x, z = [list(s) for s in carry]
            for k in range(unroll):
                t = i * unroll + k
                ut = at(u_s, t)[...]
                ob = at(o_s, rows - 1 - t)[...]
                for j in range(wide):
                    x[j] = a[j] * x[j] + ut
                    z[j] = a[j] * z[j] + ob
            return tuple(x), tuple(z)

        done = lax.fori_loop(0, rows // unroll, step, ((zero,) * wide,) * 2)
        for j in range(wide):
            sub = slice((j % per) * SUB, (j % per + 1) * SUB)
            for f in range(2):
                ends[c * (wide // per) + j // per, f, sub, :] = done[f][j]

    def summarise(turn):
        c = chunk_of(turn)
        a = [a_s[mode_rows(c * batch + j), :] for j in range(batch)]

        def step(i, carry):
            x, y, r, e, z, v = [list(s) for s in carry]
            for k in range(unroll):
                t = i * unroll + k
                ut = at(u_s, t)[...]
                ot = at(o_s, t)[...]
                ob = at(o_s, rows - 1 - t)[...]
                for j in range(batch):
                    y[j] = a[j] * (y[j] + x[j])
                    x[j] = a[j] * x[j] + ut
                    r[j] = r[j] + ot * x[j]
                    e[j] = e[j] + ot * y[j]
                    z[j] = a[j] * z[j] + ob
                    v[j] = a[j] * v[j] + z[j]
            return tuple(tuple(s) for s in (x, y, r, e, z, v))

        x, y, r, e, z, v = lax.fori_loop(
            0, rows // unroll, step, tuple((zero,) * batch for _ in range(6)))
        for j in range(batch):
            q = c * owners_per + j // per
            sub = slice((j % per) * SUB, (j % per + 1) * SUB)
            for f, value in enumerate((y, r, e, v)):
                sums[q, f, sub, :] = value[j]

    def send_chunk(copy, turn):
        for b in range(owners_per):
            q = chunk_of(turn) * owners_per + b

            @pl.when(q != me)
            def _():
                copy(q).start()

    @pl.loop(0, modes // wide)
    def _(c):
        edges(c)

    pl.semaphore_wait(barrier, n - 1)
    each_other(own, lambda q: ends_to(q).start())

    @pl.loop(0, turns)
    def _(turn):
        summarise(turn)
        send_chunk(sums_to, turn)

    def total(terms):
        while len(terms) > 1:
            terms = [x + y for x, y in zip(terms[::2], terms[1::2])]
        return terms[0]

    skip = jnp.concatenate([skip_ref[:, g * LANES:(g + 1) * LANES] for g in range(groups)], axis=0)

    def scan(src, dst, place):
        def step(i, x):
            x = list(x)
            here = [place(i * unroll + k) for k in range(unroll)]
            terms = [at(src, t)[...] for t in here]
            sums = []
            for term in terms:
                x = [a_s[mode_rows(m), :] * x[m] + term for m in range(modes)]
                sums.append(skip * term + total([w_s[mode_rows(m), :] * x[m] for m in range(modes)]))
            for t, value in zip(here, sums):
                at(dst, t)[...] = value
            return tuple(x)

        lax.fori_loop(0, rows // unroll, step, (zero,) * modes)

    def forward(t):
        return t

    def backward(t):
        return rows - 1 - t

    few = n <= 16
    none = jnp.zeros((slab, LANES), f32)

    def owned():
        mine = pl.ds(pl.multiple_of(lax.rem(me, own) * slab, slab), slab)
        d = d_s[mine, :]
        return d, a_s[mine, :], jnp.exp(-float(rows) * d)

    @pl.when(me < own)
    def _():
        _, _, at_end = owned()
        got_ends[me] = ends[me]
        each_other(n, lambda r: ends_from(r).wait_recv())

        def carry_on(i, carry):
            x, z = carry
            r = n - 1 - i
            starts[i, 0] = x
            starts[r, 1] = z
            return at_end * x + got_ends[i, 0], at_end * z + got_ends[r, 1]

        lax.fori_loop(0, n, carry_on, (none, none), unroll=few)
        each_other(n, lambda r: starts_to(r).start())
        got_starts[me] = starts[me]

    scan(u_s, conv_s, forward)
    scan(o_s, adj_s, backward)

    @pl.when(me < own)
    def _():
        d, a, at_end = owned()
        got_sums[me] = sums[me]
        each_other(n, lambda r: sums_from(r).wait_recv())

        def gather(r, carry):
            y, rt, dt = carry
            x, z = starts[r, 0], got_ends[r, 1]
            rt = rt + got_sums[r, 1] + a * (x * z)
            dt = dt + got_sums[r, 2] + a * (got_sums[r, 3] * x + z * y)
            y = at_end * (y + float(rows) * x) + got_sums[r, 0]
            return y, rt, dt

        _, rt, dt = lax.fori_loop(0, n, gather, (none,) * 3, unroll=few)
        totals[0] = rt / seq
        totals[1] = dt * d / seq
        each_other(n, lambda r: totals_to(r).start())
        got_totals[me] = totals[...]

    each_other(own, lambda q: starts_from(q).wait_recv())

    def decay_from(field, src, dst, place):
        def start(m):
            sub = slice((m % per) * SUB, (m % per + 1) * SUB)
            return w_s[mode_rows(m), :] * a_s[mode_rows(m), :] * got_starts[m // per, field, sub, :]

        def step(i, p):
            p = list(p)
            here = [place(i * unroll + k) for k in range(unroll)]
            local = [at(src, t)[...] for t in here]
            sums = []
            for value in local:
                sums.append(value + total(p))
                p = [a_s[mode_rows(m), :] * p[m] for m in range(modes)]
            for t, value in zip(here, sums):
                at(dst, t)[...] = value
            return tuple(p)

        lax.fori_loop(0, rows // unroll, step, tuple(start(m) for m in range(modes)))

    decay_from(0, conv_s, conv_out, forward)
    decay_from(1, adj_s, adj_out, backward)
    each_other(own, lambda q: totals_from(q).wait_recv())
    for q in range(own):
        rt_s[q * slab:(q + 1) * slab, :] = got_totals[q, 0]
        dt_s[q * slab:(q + 1) * slab, :] = got_totals[q, 1]

    each_other(own, lambda q: ends_to(q).wait_send())
    each_other(own, lambda q: sums_to(q).wait_send())

    @pl.when(me < own)
    def _():
        each_other(n, lambda r: starts_to(r).wait_send())
        each_other(n, lambda r: totals_to(r).wait_send())


def finish(
    conv_ref, adj_ref, rt_ref, dt_ref, k_ref, v_ref, g_ref,
    qg_hbm, kg_hbm, vg_hbm, rg_hbm, dg_hbm,
    qg_ref, kg_ref, vg_ref, rg_ref, dg_ref, outs,
):
    rows, cols = k_ref.shape
    modes = rg_ref.shape[0]
    groups = cols // LANES
    stores = [
        pltpu.make_async_copy(src, dst, outs.at[i])
        for i, (src, dst) in enumerate((
            (rg_ref, rg_hbm), (dg_ref, dg_hbm), (qg_ref, qg_hbm), (kg_ref, kg_hbm), (vg_ref, vg_hbm)))
    ]
    for g in range(groups):
        lanes = slice(g * LANES, (g + 1) * LANES)
        rg_ref[:, lanes] = rt_ref[pl.ds(g, modes, stride=groups), :]
        dg_ref[:, lanes] = dt_ref[pl.ds(g, modes, stride=groups), :]
    stores[0].start()
    stores[1].start()
    for g in range(groups):
        lanes = slice(g * LANES, (g + 1) * LANES)
        block = slice(g * rows, (g + 1) * rows)
        qg_ref[:, lanes] = (g_ref[:, lanes].astype(f32) * conv_ref[block, :]).astype(qg_ref.dtype)
    stores[2].start()
    for g in range(groups):
        lanes = slice(g * LANES, (g + 1) * LANES)
        block = slice(g * rows, (g + 1) * rows)
        kg_ref[:, lanes] = (adj_ref[block, :] * v_ref[:, lanes].astype(f32)).astype(kg_ref.dtype)
        vg_ref[:, lanes] = (adj_ref[block, :] * k_ref[:, lanes].astype(f32)).astype(vg_ref.dtype)
    stores[3].start()
    stores[4].start()
    for store in stores:
        store.wait()


def body(n, queries, keys, values, grad_out, residues, decays, skip):
    rows, cols = queries.shape
    modes = residues.shape[1]
    own = min(n, modes)
    slab = modes * cols // LANES // own
    vmem = pl.BlockSpec(memory_space=pltpu.VMEM)
    hbm = pl.BlockSpec(memory_space=pltpu.HBM)
    size = (rows * cols // LANES, LANES)
    held = (modes * cols // LANES, LANES)
    field = pltpu.VMEM(size, f32)
    table = pltpu.VMEM(held, f32)
    gate = pltpu.VMEM((rows, cols), jnp.bfloat16)
    wide = pltpu.VMEM((modes, cols), f32)
    conv, adj, rt, dt = pl.pallas_call(
        functools.partial(kernel, n, own),
        out_shape=tuple(jax.ShapeDtypeStruct(s, f32) for s in (size, size, held, held)),
        in_specs=[hbm] * 7,
        out_specs=(vmem,) * 4,
        scratch_shapes=[
            gate, gate, gate, gate, wide, wide, pltpu.VMEM((1, cols), f32),
            pltpu.SemaphoreType.DMA((7,)),
            field, field, field, field,
            table, table, table,
            pltpu.VMEM((own, 2, slab, LANES), f32),
            pltpu.VMEM((n, 2, slab, LANES), f32),
            pltpu.VMEM((own, 4, slab, LANES), f32),
            pltpu.VMEM((n, 4, slab, LANES), f32),
            pltpu.VMEM((n, 2, slab, LANES), f32),
            pltpu.VMEM((own, 2, slab, LANES), f32),
            pltpu.VMEM((2, slab, LANES), f32),
            pltpu.VMEM((own, 2, slab, LANES), f32),
        ] + [
            pltpu.SemaphoreType.DMA((count,)) for count in (own, n, own, n, n, own, n, own)
        ],
        compiler_params=pltpu.CompilerParams(
            collective_id=0, has_side_effects=True, vmem_limit_bytes=24 * 1024 * 1024
        ),
    )(*[pltpu.with_memory_space_constraint(x, pltpu.HBM) for x in (queries, keys, values, grad_out, residues.T, decays.T, skip.reshape(1, cols))])
    grads = jax.ShapeDtypeStruct((rows, cols), jnp.bfloat16)
    sums = jax.ShapeDtypeStruct((modes, cols), f32)
    qg, kg, vg, rg, dg = pl.pallas_call(
        finish,
        out_shape=(grads, grads, grads, sums, sums),
        in_specs=[vmem] * 7,
        out_specs=(hbm,) * 5,
        scratch_shapes=[gate, gate, gate, wide, wide, pltpu.SemaphoreType.DMA((5,))],
        compiler_params=pltpu.CompilerParams(vmem_limit_bytes=16 * 1024 * 1024),
    )(conv, adj, rt, dt, keys, values, grad_out)
    return qg, kg, vg, rg.T, dg.T


def solution(mesh):
    return jax.shard_map(
        functools.partial(body, mesh.shape["ctx"]),
        mesh=mesh,
        in_specs=(
            P("ctx", "ch"), P("ctx", "ch"), P("ctx", "ch"), P("ctx", "ch"),
            P("ch", None), P("ch", None), P("ch"),
        ),
        out_specs=(P("ctx", "ch"), P("ctx", "ch"), P("ctx", "ch"), P("ch", None), P("ch", None)),
        check_vma=False,
    )
```

```python
import functools

import jax
import jax.numpy as jnp
from jax import lax
from jax.experimental import pallas as pl
from jax.experimental.pallas import tpu as pltpu
from jax.sharding import PartitionSpec as P

LANES = 128
SUB = 8
MESH = pl.DeviceIdType.MESH
f32 = jnp.float32


def kernel(
    n, own, q_hbm, k_hbm, v_hbm, g_hbm, res_hbm, dec_hbm, skip_hbm,
    conv_out, adj_out, rt_s, dt_s,
    q_ref, k_ref, v_ref, g_ref, res_ref, dec_ref, skip_ref, ins,
    u_s, o_s, conv_s, adj_s, d_s, a_s, w_s,
    ends, got_ends, sums, got_sums, starts, got_starts, totals, got_totals,
    ends_out, ends_in, sums_out, sums_in, starts_out, starts_in, totals_out, totals_in,
):
    rows, cols = q_ref.shape
    modes = res_ref.shape[0]
    groups = cols // LANES
    seq = rows * n
    slab = modes * groups // own
    per = slab // SUB
    me = lax.axis_index("ctx")

    barrier = pltpu.get_barrier_semaphore()
    fetches = [
        pltpu.make_async_copy(src, dst, ins.at[i])
        for i, (src, dst) in enumerate((
            (dec_hbm, dec_ref), (k_hbm, k_ref), (v_hbm, v_ref), (q_hbm, q_ref),
            (g_hbm, g_ref), (res_hbm, res_ref), (skip_hbm, skip_ref)))
    ]
    for fetch in fetches:
        fetch.start()

    @pl.loop(0, n)
    def _(peer):
        @pl.when(peer != me)
        def _():
            pl.semaphore_signal(barrier, inc=1, device_id={"ctx": peer}, device_id_type=MESH)

    for fetch in fetches:
        fetch.wait()
    for g in range(groups):
        lanes = slice(g * LANES, (g + 1) * LANES)
        block = slice(g * rows, (g + 1) * rows)
        u_s[block, :] = k_ref[:, lanes].astype(f32) * v_ref[:, lanes].astype(f32)
        o_s[block, :] = q_ref[:, lanes].astype(f32) * g_ref[:, lanes].astype(f32)
        d = dec_ref[:, lanes]
        d_s[pl.ds(g, modes, stride=groups), :] = d
        a_s[pl.ds(g, modes, stride=groups), :] = jnp.exp(-d)
        w_s[pl.ds(g, modes, stride=groups), :] = res_ref[:, lanes]

    def at(ref, t):
        return ref.at[pl.ds(t, SUB, stride=rows), :]

    def mode_rows(m):
        return pl.ds(pl.multiple_of(m * SUB, SUB), SUB)

    def link(src, dst, sent, landed, peer):
        return pltpu.make_async_remote_copy(
            src_ref=src, dst_ref=dst, send_sem=sent, recv_sem=landed,
            device_id={"ctx": peer}, device_id_type=MESH)

    def each_other(count, act):
        @pl.loop(0, count)
        def _(i):
            @pl.when(i != me)
            def _():
                act(i)

    def ends_to(q):
        return link(ends.at[q], got_ends.at[me], ends_out.at[q], ends_in.at[me], q)

    def ends_from(r):
        return link(ends.at[0], got_ends.at[r], ends_out.at[0], ends_in.at[r], r)

    def sums_to(q):
        return link(sums.at[q], got_sums.at[me], sums_out.at[q], sums_in.at[me], q)

    def sums_from(r):
        return link(sums.at[0], got_sums.at[r], sums_out.at[0], sums_in.at[r], r)

    def starts_to(r):
        return link(starts.at[r], got_starts.at[me], starts_out.at[r], starts_in.at[me], r)

    def starts_from(q):
        return link(starts.at[0], got_starts.at[q], starts_out.at[0], starts_in.at[q], q)

    def totals_to(r):
        return link(totals, got_totals.at[me], totals_out.at[r], totals_in.at[me], r)

    def totals_from(q):
        return link(totals, got_totals.at[q], totals_out.at[0], totals_in.at[q], q)

    zero = jnp.zeros((SUB, LANES), f32)
    batch = 4
    turns = modes // batch
    owners_per = batch // per
    unroll = 16

    def chunk_of(turn):
        return lax.rem(turn + me // owners_per, turns)

    def summarise(turn):
        c = chunk_of(turn)
        a = [a_s[mode_rows(c * batch + j), :] for j in range(batch)]

        def step(i, carry):
            x, y, r, e, z, v = [list(s) for s in carry]
            for k in range(unroll):
                t = i * unroll + k
                ut = at(u_s, t)[...]
                ot = at(o_s, t)[...]
                ob = at(o_s, rows - 1 - t)[...]
                for j in range(batch):
                    y[j] = a[j] * (y[j] + x[j])
                    x[j] = a[j] * x[j] + ut
                    r[j] = r[j] + ot * x[j]
                    e[j] = e[j] + ot * y[j]
                    z[j] = a[j] * z[j] + ob
                    v[j] = a[j] * v[j] + z[j]
            return tuple(tuple(s) for s in (x, y, r, e, z, v))

        x, y, r, e, z, v = lax.fori_loop(
            0, rows // unroll, step, tuple((zero,) * batch for _ in range(6)))
        for j in range(batch):
            q = c * owners_per + j // per
            sub = slice((j % per) * SUB, (j % per + 1) * SUB)
            for f, value in enumerate((x, z)):
                ends[q, f, sub, :] = value[j]
            for f, value in enumerate((y, r, e, v)):
                sums[q, f, sub, :] = value[j]

    def send_chunk(copy, turn):
        for b in range(owners_per):
            q = chunk_of(turn) * owners_per + b

            @pl.when(q != me)
            def _():
                copy(q).start()

    early = 1

    @pl.loop(0, early)
    def _(turn):
        summarise(turn)

    pl.semaphore_wait(barrier, n - 1)

    @pl.loop(0, early)
    def _(turn):
        send_chunk(ends_to, turn)

    if early < turns:
        @pl.loop(early, turns)
        def _(turn):
            summarise(turn)
            send_chunk(ends_to, turn)

    @pl.loop(0, turns)
    def _(turn):
        send_chunk(sums_to, turn)

    def total(terms):
        while len(terms) > 1:
            terms = [x + y for x, y in zip(terms[::2], terms[1::2])]
        return terms[0]

    skip = jnp.concatenate([skip_ref[:, g * LANES:(g + 1) * LANES] for g in range(groups)], axis=0)

    def scan(src, dst, place):
        def step(i, x):
            x = list(x)
            here = [place(i * unroll + k) for k in range(unroll)]
            terms = [at(src, t)[...] for t in here]
            sums = []
            for term in terms:
                x = [a_s[mode_rows(m), :] * x[m] + term for m in range(modes)]
                sums.append(skip * term + total([w_s[mode_rows(m), :] * x[m] for m in range(modes)]))
            for t, value in zip(here, sums):
                at(dst, t)[...] = value
            return tuple(x)

        lax.fori_loop(0, rows // unroll, step, (zero,) * modes)

    def forward(t):
        return t

    def backward(t):
        return rows - 1 - t

    scan(u_s, conv_s, forward)
    few = n <= 16
    none = jnp.zeros((slab, LANES), f32)

    def owned():
        mine = pl.ds(pl.multiple_of(lax.rem(me, own) * slab, slab), slab)
        d = d_s[mine, :]
        return d, a_s[mine, :], jnp.exp(-float(rows) * d)

    @pl.when(me < own)
    def _():
        _, _, at_end = owned()
        got_ends[me] = ends[me]
        each_other(n, lambda r: ends_from(r).wait_recv())

        def carry_on(i, carry):
            x, z = carry
            r = n - 1 - i
            starts[i, 0] = x
            starts[r, 1] = z
            return at_end * x + got_ends[i, 0], at_end * z + got_ends[r, 1]

        lax.fori_loop(0, n, carry_on, (none, none), unroll=few)
        each_other(n, lambda r: starts_to(r).start())
        got_starts[me] = starts[me]

    scan(o_s, adj_s, backward)

    @pl.when(me < own)
    def _():
        d, a, at_end = owned()
        got_sums[me] = sums[me]
        each_other(n, lambda r: sums_from(r).wait_recv())

        def gather(r, carry):
            y, rt, dt = carry
            x, z = starts[r, 0], got_ends[r, 1]
            rt = rt + got_sums[r, 1] + a * (x * z)
            dt = dt + got_sums[r, 2] + a * (got_sums[r, 3] * x + z * y)
            y = at_end * (y + float(rows) * x) + got_sums[r, 0]
            return y, rt, dt

        _, rt, dt = lax.fori_loop(0, n, gather, (none,) * 3, unroll=few)
        totals[0] = rt / seq
        totals[1] = dt * d / seq
        each_other(n, lambda r: totals_to(r).start())
        got_totals[me] = totals[...]

    each_other(own, lambda q: starts_from(q).wait_recv())

    def decay_from(field, src, dst, place):
        def start(m):
            sub = slice((m % per) * SUB, (m % per + 1) * SUB)
            return w_s[mode_rows(m), :] * a_s[mode_rows(m), :] * got_starts[m // per, field, sub, :]

        def step(i, p):
            p = list(p)
            here = [place(i * unroll + k) for k in range(unroll)]
            local = [at(src, t)[...] for t in here]
            sums = []
            for value in local:
                sums.append(value + total(p))
                p = [a_s[mode_rows(m), :] * p[m] for m in range(modes)]
            for t, value in zip(here, sums):
                at(dst, t)[...] = value
            return tuple(p)

        lax.fori_loop(0, rows // unroll, step, tuple(start(m) for m in range(modes)))

    decay_from(0, conv_s, conv_out, forward)
    decay_from(1, adj_s, adj_out, backward)
    each_other(own, lambda q: totals_from(q).wait_recv())
    for q in range(own):
        rt_s[q * slab:(q + 1) * slab, :] = got_totals[q, 0]
        dt_s[q * slab:(q + 1) * slab, :] = got_totals[q, 1]

    each_other(own, lambda q: ends_to(q).wait_send())
    each_other(own, lambda q: sums_to(q).wait_send())

    @pl.when(me < own)
    def _():
        each_other(n, lambda r: starts_to(r).wait_send())
        each_other(n, lambda r: totals_to(r).wait_send())


def finish(
    conv_ref, adj_ref, rt_ref, dt_ref, k_ref, v_ref, g_ref,
    qg_hbm, kg_hbm, vg_hbm, rg_hbm, dg_hbm,
    qg_ref, kg_ref, vg_ref, rg_ref, dg_ref, outs,
):
    rows, cols = k_ref.shape
    modes = rg_ref.shape[0]
    groups = cols // LANES
    stores = [
        pltpu.make_async_copy(src, dst, outs.at[i])
        for i, (src, dst) in enumerate((
            (rg_ref, rg_hbm), (dg_ref, dg_hbm), (qg_ref, qg_hbm), (kg_ref, kg_hbm), (vg_ref, vg_hbm)))
    ]
    for g in range(groups):
        lanes = slice(g * LANES, (g + 1) * LANES)
        rg_ref[:, lanes] = rt_ref[pl.ds(g, modes, stride=groups), :]
        dg_ref[:, lanes] = dt_ref[pl.ds(g, modes, stride=groups), :]
    stores[0].start()
    stores[1].start()
    for g in range(groups):
        lanes = slice(g * LANES, (g + 1) * LANES)
        block = slice(g * rows, (g + 1) * rows)
        qg_ref[:, lanes] = (g_ref[:, lanes].astype(f32) * conv_ref[block, :]).astype(qg_ref.dtype)
    stores[2].start()
    for g in range(groups):
        lanes = slice(g * LANES, (g + 1) * LANES)
        block = slice(g * rows, (g + 1) * rows)
        kg_ref[:, lanes] = (adj_ref[block, :] * v_ref[:, lanes].astype(f32)).astype(kg_ref.dtype)
        vg_ref[:, lanes] = (adj_ref[block, :] * k_ref[:, lanes].astype(f32)).astype(vg_ref.dtype)
    stores[3].start()
    stores[4].start()
    for store in stores:
        store.wait()


def body(n, queries, keys, values, grad_out, residues, decays, skip):
    rows, cols = queries.shape
    modes = residues.shape[1]
    own = min(n, modes)
    slab = modes * cols // LANES // own
    vmem = pl.BlockSpec(memory_space=pltpu.VMEM)
    hbm = pl.BlockSpec(memory_space=pltpu.HBM)
    size = (rows * cols // LANES, LANES)
    held = (modes * cols // LANES, LANES)
    field = pltpu.VMEM(size, f32)
    table = pltpu.VMEM(held, f32)
    gate = pltpu.VMEM((rows, cols), jnp.bfloat16)
    wide = pltpu.VMEM((modes, cols), f32)
    conv, adj, rt, dt = pl.pallas_call(
        functools.partial(kernel, n, own),
        out_shape=tuple(jax.ShapeDtypeStruct(s, f32) for s in (size, size, held, held)),
        in_specs=[hbm] * 7,
        out_specs=(vmem,) * 4,
        scratch_shapes=[
            gate, gate, gate, gate, wide, wide, pltpu.VMEM((1, cols), f32),
            pltpu.SemaphoreType.DMA((7,)),
            field, field, field, field,
            table, table, table,
            pltpu.VMEM((own, 2, slab, LANES), f32),
            pltpu.VMEM((n, 2, slab, LANES), f32),
            pltpu.VMEM((own, 4, slab, LANES), f32),
            pltpu.VMEM((n, 4, slab, LANES), f32),
            pltpu.VMEM((n, 2, slab, LANES), f32),
            pltpu.VMEM((own, 2, slab, LANES), f32),
            pltpu.VMEM((2, slab, LANES), f32),
            pltpu.VMEM((own, 2, slab, LANES), f32),
        ] + [
            pltpu.SemaphoreType.DMA((count,)) for count in (own, n, own, n, n, own, n, own)
        ],
        compiler_params=pltpu.CompilerParams(
            collective_id=0, has_side_effects=True, vmem_limit_bytes=24 * 1024 * 1024
        ),
    )(*[pltpu.with_memory_space_constraint(x, pltpu.HBM) for x in (queries, keys, values, grad_out, residues.T, decays.T, skip.reshape(1, cols))])
    grads = jax.ShapeDtypeStruct((rows, cols), jnp.bfloat16)
    sums = jax.ShapeDtypeStruct((modes, cols), f32)
    qg, kg, vg, rg, dg = pl.pallas_call(
        finish,
        out_shape=(grads, grads, grads, sums, sums),
        in_specs=[vmem] * 7,
        out_specs=(hbm,) * 5,
        scratch_shapes=[gate, gate, gate, wide, wide, pltpu.SemaphoreType.DMA((5,))],
        compiler_params=pltpu.CompilerParams(vmem_limit_bytes=16 * 1024 * 1024),
    )(conv, adj, rt, dt, keys, values, grad_out)
    return qg, kg, vg, rg.T, dg.T


def solution(mesh):
    return jax.shard_map(
        functools.partial(body, mesh.shape["ctx"]),
        mesh=mesh,
        in_specs=(
            P("ctx", "ch"), P("ctx", "ch"), P("ctx", "ch"), P("ctx", "ch"),
            P("ch", None), P("ch", None), P("ch"),
        ),
        out_specs=(P("ctx", "ch"), P("ctx", "ch"), P("ctx", "ch"), P("ch", None), P("ch", None)),
        check_vma=False,
    )
```
